1024 devices in a mesh: term: 128 (over y, z), blk: 8 (over x, core).
Axes of the slice: x: 4, y: 8, z: 16, core: 2. Of those that a mesh axis runs over, the one named last changes fastest.
Arguments:
- psi: bfloat16 [2, 8, 512, 448], P(None, 'blk'), may hold values from -6 to 6
- left_env: bfloat16 [128, 8, 512, 512], P('term', 'blk'), may hold values from -0.03125 to 0.03125
- right_env: bfloat16 [128, 8, 448, 448], P('term', 'blk'), may hold values from -0.375 to 0.375
- source: int32 [128, 8], P('term', 'blk'), may hold values from 0 to 7
- left_size: int32 [8], replicated, may hold values from 64 to 512
- right_size: int32 [8], replicated, may hold values from 64 to 448
Outputs:
- sigma: float32 [2, 8, 512, 448], P(None, 'blk', 'term')
The draws below stay inside these ranges and needn't reach their ends.
All inputs are finite; a program needn't handle non-finite values.
Results may differ from the reference program's by a relative error of at most 0.0029.
Values may be sent and summed in bfloat16 or wider, within the bound.
No kernel may reach another device: no remote copies, remote signals or barrier semaphores. Data moves between devices by JAX's collectives and lax.ppermute only.
A program may use at most 32 MiB of HBM per device.

```python
import jax
import jax.numpy as jnp
from jax import lax

BL = 512
BR = 448
VECS = 2
TERMS = 128
NBLK = 8


def draw_left_size(key, part):
    key = jax.random.fold_in(key, 11)
    first, second = jax.random.split(key)
    values = jax.random.randint(first, (NBLK,), BL // 8, BL + 1)
    place = jax.random.randint(second, (), 0, NBLK)
    return values.at[place].set(BL).astype(jnp.int32)


def draw_right_size(key, part):
    key = jax.random.fold_in(key, 23)
    first, second = jax.random.split(key)
    values = jax.random.randint(first, (NBLK,), BR // 7, BR + 1)
    place = jax.random.randint(second, (), 0, NBLK)
    return values.at[place].set(BR).astype(jnp.int32)


def set_ends(values, own_key, low, largest):
    spot = [jax.random.randint(jax.random.fold_in(own_key, axis), (), 0, length) for axis, length in enumerate(values.shape)]
    widest = values.shape.index(max(values.shape))
    next_to = spot[:widest] + [(spot[widest] + 1) % values.shape[widest]] + spot[widest + 1:]
    return values.at[tuple(spot)].set(low).at[tuple(next_to)].set(largest)


def levels(rng, shape, cuts, smallest, high):
    level, own = 1.0, jax.random.fold_in(rng, 6)
    for axis_at, shards_of in cuts:
        draws = jnp.exp(jax.random.uniform(jax.random.fold_in(own, axis_at), (shards_of,), jnp.float32, smallest / len(cuts), high / len(cuts)))
        level = level * jnp.repeat(draws, shape[axis_at] // shards_of).reshape([-1 if axis == axis_at else 1 for axis in range(len(shape))])
    return level


def centred(rng, extent, spread, limit, pieces=(), kind=jnp.bfloat16):
    entries = jax.random.normal(rng, extent, jnp.float32) * spread
    if len(pieces) > 0:
        entries = levels(rng, extent, pieces, -0.22, 0.18) * entries
    return jnp.clip(entries, min=-limit, max=limit).astype(kind)


def setup_inputs(seed: int = 0) -> dict:
    arg_keys = jax.random.split(jax.random.key(seed), 7)
    psi = centred(arg_keys[0], (VECS, NBLK, BL, BR), 1.0, 6.0, ((1, 8),))
    left_env = centred(arg_keys[1], (TERMS, NBLK, BL, BL), (BL * TERMS // 2) ** -0.5, 0.03125, ((0, 128), (1, 8)))
    right_env = centred(arg_keys[2], (TERMS, NBLK, BR, BR), (BR // 2) ** -0.5, 0.375, ((0, 128), (1, 8)))
    source = set_ends(jax.random.randint(arg_keys[3], (TERMS, NBLK), 0, NBLK), jax.random.fold_in(arg_keys[3], 1), 0, NBLK - 1).astype(jnp.int32)
    left_size = draw_left_size(jax.random.fold_in(arg_keys[6], 71), 0)
    right_size = draw_right_size(jax.random.fold_in(arg_keys[6], 71), 0)
    return dict(psi=psi, left_env=left_env, right_env=right_env, source=source, left_size=left_size, right_size=right_size)


def reference(psi, left_env, right_env, source, left_size, right_size):
    row_ids = jnp.arange(BL, dtype=jnp.int32)
    col_ids = jnp.arange(BR, dtype=jnp.int32)

    def one_block(j):
        keep_out = (row_ids < left_size[j])[:, None] & (col_ids < right_size[j])[None, :]

        def add_term(total, t):
            s = source[t, j]
            block = lax.dynamic_index_in_dim(psi, s, 1, keepdims=False)
            keep_in = (row_ids < left_size[s])[:, None] & (col_ids < right_size[s])[None, :]
            block = jnp.where(keep_in[None], block, jnp.zeros_like(block))
            left = lax.dynamic_index_in_dim(lax.dynamic_index_in_dim(left_env, t, 0, keepdims=False), j, 0, keepdims=False)
            right = lax.dynamic_index_in_dim(lax.dynamic_index_in_dim(right_env, t, 0, keepdims=False), j, 0, keepdims=False)
            middle = jnp.einsum('ab,vbc->vac', left.astype(jnp.float32), block.astype(jnp.float32)).astype(jnp.bfloat16)
            result = jnp.einsum('vac,cd->vad', middle.astype(jnp.float32), right.astype(jnp.float32))
            return total + jnp.where(keep_out[None], result, jnp.zeros_like(result)), None

        start = jnp.zeros((VECS, BL, BR), jnp.float32)
        total, unused = lax.scan(add_term, start, jnp.arange(TERMS, dtype=jnp.int32))
        return total

    sigma = lax.map(one_block, jnp.arange(NBLK, dtype=jnp.int32))
    return jnp.transpose(sigma, (1, 0, 2, 3))
```

```python
import jax
import jax.numpy as jnp
from jax import lax
from jax.experimental import pallas as pl
from jax.experimental.pallas import tpu as pltpu
from jax.sharding import Mesh, PartitionSpec as P

VECTORS = 2


def pick_kernel(wanted, have, out):
    out[...] = have[...]


def pick(have, wanted):
    slots, rows, cols = have.shape
    return pl.pallas_call(
        pick_kernel,
        out_shape=jax.ShapeDtypeStruct((slots, rows, cols), have.dtype),
        grid_spec=pltpu.PrefetchScalarGridSpec(
            num_scalar_prefetch=1,
            grid=(slots,),
            in_specs=[pl.BlockSpec((1, rows, cols), lambda i, wanted: (wanted[i], 0, 0))],
            out_specs=pl.BlockSpec((1, rows, cols), lambda i, wanted: (i, 0, 0)),
        ),
        name="pick",
    )(wanted, have)


def apply_kernel(order, source, left_size, right_size, block, left, right, out):
    rows = left.shape[0]
    cols = right.shape[0]
    here = lax.axis_index("x") * lax.axis_size("core") + lax.axis_index("core")
    target = source[0, 0]
    out_row = lax.broadcasted_iota(jnp.int32, (rows, rows), 0)
    in_row = lax.broadcasted_iota(jnp.int32, (rows, rows), 1)
    keep = (order(out_row) == in_row) & (in_row < left_size[here])
    permute = jnp.where(keep, 1.0, 0.0).astype(left.dtype)
    live = lax.broadcasted_iota(jnp.int32, (rows, rows), 1) < left_size[target]
    lefts = jnp.where(live, left[...], jnp.zeros_like(left))
    lefts = jnp.dot(permute, lefts, preferred_element_type=jnp.float32).astype(left.dtype)
    row = lax.broadcasted_iota(jnp.int32, (cols, cols), 0)
    col = lax.broadcasted_iota(jnp.int32, (cols, cols), 1)
    live = (row < right_size[target]) & (col < right_size[here])
    rights = jnp.where(live, right[...], jnp.zeros_like(right))
    results = []
    for v in range(VECTORS):
        middle = lax.dot_general(
            lefts,
            block[v * cols : (v + 1) * cols, :],
            (((1,), (1,)), ((), ())),
            preferred_element_type=jnp.float32,
        ).astype(left.dtype)
        results.append(jnp.dot(middle, rights, preferred_element_type=jnp.float32))
    out[...] = jnp.concatenate(results, axis=1).astype(out.dtype)


def apply(order, source, left_size, right_size, block, left, right):
    rows = left.shape[0]
    cols = right.shape[0]
    smem = pl.BlockSpec(memory_space=pltpu.SMEM)
    vmem = pl.BlockSpec(memory_space=pltpu.VMEM)
    return pl.pallas_call(
        lambda *refs: apply_kernel(order, *refs),
        out_shape=jax.ShapeDtypeStruct((rows, VECTORS * cols), left.dtype),
        in_specs=[smem] * 3 + [vmem] * 3,
        out_specs=vmem,
        compiler_params=pltpu.CompilerParams(vmem_limit_bytes=32 * 1024 * 1024),
        name="apply",
    )(source, left_size, right_size, block, left, right)


def local(psi, left_env, right_env, source, left_size, right_size):
    size = lax.axis_size
    rows = psi.shape[2]
    cols = psi.shape[3]
    near = size("yl") * size("zl")
    far = size("yh") * size("zh")
    each = rows // (near * far)

    asked = lax.optimization_barrier(jnp.broadcast_to(source, (8, 128)))
    asked = lax.optimization_barrier(lax.all_gather(asked, ("core", "yl", "zl")))
    wanted = asked[:, 0, 0]

    share = cols // near
    part = lax.axis_index("yl") * size("zl") + lax.axis_index("zl")
    turned = jnp.transpose(psi[:, 0], (0, 2, 1))
    mine = lax.dynamic_slice_in_dim(turned, part * share, share, 1)
    sends = jnp.broadcast_to(mine[None], (size("x"),) + mine.shape)
    sends = sends.reshape(-1, share, rows)
    have = lax.all_to_all(sends, ("x", "core"), 0, 0)
    block = lax.all_to_all(pick(have, wanted), ("core", "yl", "zl"), 0, 0)
    block = block.reshape(VECTORS * cols, rows)

    def order(p):
        unit, last = p // each, p % each
        zh, unit = unit % size("zh"), unit // size("zh")
        yh, unit = unit % size("yh"), unit // size("yh")
        zl, yl = unit % size("zl"), unit // size("zl")
        term = ((yh * size("yl") + yl) * size("zh") + zh) * size("zl") + zl
        return term * each + last

    result = apply(order, source, left_size, right_size, block, left_env[0, 0], right_env[0, 0])
    result = result.reshape(near, rows // near, VECTORS * cols)
    got = lax.all_to_all(result, ("yl", "zl"), 0, 0)
    total = jnp.sum(got.astype(jnp.float32), axis=0).astype(jnp.bfloat16)
    got = lax.all_to_all(total.reshape(far, each, VECTORS * cols), ("yh", "zh"), 0, 0)
    total = jnp.sum(got.astype(jnp.float32), axis=0)
    return jnp.transpose(total.reshape(each, VECTORS, cols), (1, 0, 2))[:, None]


def solution(mesh):
    y, z = 8, 16
    shape = (y // 2, 2, z // 2, 2, 4, 2)
    fine = Mesh(mesh.devices.reshape(shape), ("yh", "yl", "zh", "zl", "x", "core"))
    term = ("yh", "yl", "zh", "zl")
    blk = ("x", "core")
    return jax.shard_map(
        local,
        mesh=fine,
        in_specs=(P(None, blk), P(term, blk), P(term, blk), P(term, blk), P(), P()),
        out_specs=P(None, blk, term),
        check_vma=False,
    )
```

```python
import jax
import jax.numpy as jnp
from jax import lax
from jax.experimental import pallas as pl
from jax.experimental.pallas import tpu as pltpu
from jax.sharding import Mesh, PartitionSpec as P

VECTORS = 2


def pick_kernel(wanted, have, out):
    for i in range(out.shape[0]):
        out[i] = have[wanted[i]]


def pick(have, wanted):
    return pl.pallas_call(
        pick_kernel,
        out_shape=jax.ShapeDtypeStruct(have.shape, have.dtype),
        in_specs=[
            pl.BlockSpec(memory_space=pltpu.SMEM),
            pl.BlockSpec(memory_space=pltpu.VMEM),
        ],
        out_specs=pl.BlockSpec(memory_space=pltpu.VMEM),
        compiler_params=pltpu.CompilerParams(vmem_limit_bytes=16 * 1024 * 1024),
        name="pick",
    )(wanted, have)


def apply_kernel(order, source, left_size, right_size, block, left, right, out):
    rows = left.shape[0]
    cols = right.shape[0]
    here = lax.axis_index("x") * lax.axis_size("core") + lax.axis_index("core")
    target = source[0, 0]
    out_row = lax.broadcasted_iota(jnp.int32, (rows, rows), 0)
    in_row = lax.broadcasted_iota(jnp.int32, (rows, rows), 1)
    keep = (order(out_row) == in_row) & (in_row < left_size[here])
    permute = jnp.where(keep, 1.0, 0.0).astype(left.dtype)
    live = lax.broadcasted_iota(jnp.int32, (rows, rows), 1) < left_size[target]
    lefts = jnp.where(live, left[...], jnp.zeros_like(left))
    lefts = jnp.dot(permute, lefts, preferred_element_type=jnp.float32).astype(left.dtype)
    row = lax.broadcasted_iota(jnp.int32, (cols, cols), 0)
    col = lax.broadcasted_iota(jnp.int32, (cols, cols), 1)
    live = (row < right_size[target]) & (col < right_size[here])
    rights = jnp.where(live, right[...], jnp.zeros_like(right))
    results = []
    for v in range(VECTORS):
        middle = lax.dot_general(
            lefts,
            block[v * cols : (v + 1) * cols, :],
            (((1,), (1,)), ((), ())),
            preferred_element_type=jnp.float32,
        ).astype(left.dtype)
        results.append(jnp.dot(middle, rights, preferred_element_type=jnp.float32))
    out[...] = jnp.concatenate(results, axis=1).astype(out.dtype)


def apply(order, source, left_size, right_size, block, left, right):
    rows = left.shape[0]
    cols = right.shape[0]
    smem = pl.BlockSpec(memory_space=pltpu.SMEM)
    vmem = pl.BlockSpec(memory_space=pltpu.VMEM)
    return pl.pallas_call(
        lambda *refs: apply_kernel(order, *refs),
        out_shape=jax.ShapeDtypeStruct((rows, VECTORS * cols), left.dtype),
        in_specs=[smem] * 3 + [vmem] * 3,
        out_specs=vmem,
        compiler_params=pltpu.CompilerParams(vmem_limit_bytes=32 * 1024 * 1024),
        name="apply",
    )(source, left_size, right_size, block, left, right)


def squares():
    y, z, cores = (lax.axis_size(("yh", "yl")), lax.axis_size(("zh", "zl")), lax.axis_size("core"))
    return [
        [
            (((a - 2 * core * yl) % y) * z + (b - 2 * core * zl) % z) * cores + core
            for yl, a in enumerate((2 * yh, 2 * yh + 1))
            for zl, b in enumerate((2 * zh, 2 * zh + 1))
        ]
        for yh in range(y // 2)
        for zh in range(z // 2)
        for core in range(cores)
    ]


def local(psi, left_env, right_env, source, left_size, right_size):
    size = lax.axis_size
    rows = psi.shape[2]
    cols = psi.shape[3]
    near = size("yl") * size("zl")
    far = size("yh") * size("zh")
    each = rows // (near * far)

    share = cols // near
    part = lax.axis_index("yl") * size("zl") + lax.axis_index("zl")
    turned = jnp.transpose(psi[:, 0], (0, 2, 1))
    mine = lax.dynamic_slice_in_dim(turned, part * share, share, 1)
    sends = jnp.broadcast_to(mine[None], (size("x"),) + mine.shape)
    sends = sends.reshape(-1, share, rows)
    peers = ("core", "yl", "zl")
    slots = size("core") * near
    asked = jnp.where(jnp.arange(slots) == lax.axis_index(peers), source.reshape(1), 0)
    sends, asked = lax.optimization_barrier((sends, asked))
    have = lax.all_to_all(sends, ("x", "core"), 0, 0)
    wanted = lax.psum(asked, peers)
    block = lax.all_to_all(pick(have, wanted), peers, 0, 0)
    block = block.reshape(VECTORS * cols, rows)

    def order(p):
        unit, last = p // each, p % each
        zh, unit = unit % size("zh"), unit // size("zh")
        yh, unit = unit % size("yh"), unit // size("yh")
        zl, yl = unit % size("zl"), unit // size("zl")
        term = ((yh * size("yl") + yl) * size("zh") + zh) * size("zl") + zl
        return term * each + last

    result = apply(order, source, left_size, right_size, block, left_env[0, 0], right_env[0, 0])
    result = result.reshape(near, rows // near, VECTORS * cols)
    got = lax.all_to_all(result, ("yh", "yl", "zh", "zl", "core"), 0, 0, axis_index_groups=squares())
    total = jnp.sum(got.astype(jnp.float32), axis=0).astype(jnp.bfloat16)
    got = lax.all_to_all(total.reshape(far, each, VECTORS * cols), ("yh", "zh"), 0, 0)
    total = jnp.sum(got.astype(jnp.float32), axis=0)
    return jnp.transpose(total.reshape(each, VECTORS, cols), (1, 0, 2))[:, None]


def solution(mesh):
    y, z = 8, 16
    shape = (y // 2, 2, z // 2, 2, 4, 2)
    fine = Mesh(mesh.devices.reshape(shape), ("yh", "yl", "zh", "zl", "x", "core"))
    term = ("yh", "yl", "zh", "zl")
    blk = ("x", "core")
    return jax.shard_map(
        local,
        mesh=fine,
        in_specs=(P(None, blk), P(term, blk), P(term, blk), P(term, blk), P(), P()),
        out_specs=P(None, blk, term),
        check_vma=False,
    )
```

```python
import jax
import jax.numpy as jnp
from jax import lax
from jax.experimental import pallas as pl
from jax.experimental.pallas import tpu as pltpu
from jax.sharding import Mesh, PartitionSpec as P

VECTORS = 2


def pick_kernel(wanted, have, out):
    for i in range(out.shape[0]):
        out[i] = have[wanted[i]]


def pick(have, wanted):
    return pl.pallas_call(
        pick_kernel,
        out_shape=jax.ShapeDtypeStruct(have.shape, have.dtype),
        in_specs=[
            pl.BlockSpec(memory_space=pltpu.SMEM),
            pl.BlockSpec(memory_space=pltpu.VMEM),
        ],
        out_specs=pl.BlockSpec(memory_space=pltpu.VMEM),
        compiler_params=pltpu.CompilerParams(vmem_limit_bytes=16 * 1024 * 1024),
        name="pick",
    )(wanted, have)


def prepare_kernel(order, source, left_size, right_size, left, right, lefts, rights):
    rows = left.shape[0]
    cols = right.shape[0]
    here = lax.axis_index("x") * lax.axis_size("core") + lax.axis_index("core")
    target = source[0, 0]
    out_row = lax.broadcasted_iota(jnp.int32, (rows, rows), 0)
    in_row = lax.broadcasted_iota(jnp.int32, (rows, rows), 1)
    keep = (order(out_row) == in_row) & (in_row < left_size[here])
    permute = jnp.where(keep, 1.0, 0.0).astype(left.dtype)
    live = in_row < left_size[target]
    masked = jnp.where(live, left[...], jnp.zeros_like(left))
    lefts[...] = jnp.dot(permute, masked, preferred_element_type=jnp.float32).astype(left.dtype)
    row = lax.broadcasted_iota(jnp.int32, (cols, cols), 0)
    col = lax.broadcasted_iota(jnp.int32, (cols, cols), 1)
    live = (row < right_size[target]) & (col < right_size[here])
    rights[...] = jnp.where(live, right[...], jnp.zeros_like(right))


def prepare(order, source, left_size, right_size, left, right):
    smem = pl.BlockSpec(memory_space=pltpu.SMEM)
    vmem = pl.BlockSpec(memory_space=pltpu.VMEM)
    rows = left.shape[0]
    return pl.pallas_call(
        lambda *refs: prepare_kernel(order, *refs),
        out_shape=[jax.ShapeDtypeStruct(a.shape, a.dtype) for a in (left, right)],
        in_specs=[smem] * 3 + [vmem] * 2,
        out_specs=[vmem] * 2,
        compiler_params=pltpu.CompilerParams(vmem_limit_bytes=16 * 1024 * 1024),
        cost_estimate=pl.CostEstimate(flops=2 * rows**3, bytes_accessed=8 * rows * rows, transcendentals=0),
        name="prepare",
    )(source, left_size, right_size, left, right)


def apply_kernel(block, lefts, rights, out):
    cols = rights.shape[0]
    results = []
    for v in range(VECTORS):
        middle = lax.dot_general(
            lefts[...],
            block[v * cols : (v + 1) * cols, :],
            (((1,), (1,)), ((), ())),
            preferred_element_type=jnp.float32,
        ).astype(lefts.dtype)
        results.append(jnp.dot(middle, rights[...], preferred_element_type=jnp.float32))
    out[...] = jnp.concatenate(results, axis=1).astype(out.dtype)


def apply(block, lefts, rights):
    vmem = pl.BlockSpec(memory_space=pltpu.VMEM)
    return pl.pallas_call(
        apply_kernel,
        out_shape=jax.ShapeDtypeStruct((lefts.shape[0], VECTORS * rights.shape[1]), lefts.dtype),
        in_specs=[vmem] * 3,
        out_specs=vmem,
        compiler_params=pltpu.CompilerParams(vmem_limit_bytes=24 * 1024 * 1024),
        name="apply",
    )(block, lefts, rights)


def finish_kernel(parts, out):
    total = jnp.sum(parts[...].astype(jnp.float32), axis=0)
    cols = out.shape[-1]
    for v in range(VECTORS):
        out[v, 0] = total[:, v * cols : (v + 1) * cols]


def finish(parts):
    vmem = pl.BlockSpec(memory_space=pltpu.VMEM)
    unused, each, cols = parts.shape
    return pl.pallas_call(
        finish_kernel,
        out_shape=jax.ShapeDtypeStruct((VECTORS, 1, each, cols // VECTORS), jnp.float32),
        in_specs=[vmem],
        out_specs=vmem,
        name="finish",
    )(parts)


def squares():
    y, z, cores = (lax.axis_size(("yh", "yl")), lax.axis_size(("zh", "zl")), lax.axis_size("core"))
    return [
        [
            (((a - 2 * core * yl) % y) * z + (b - 2 * core * zl) % z) * cores + core
            for yl, a in enumerate((2 * yh, 2 * yh + 1))
            for zl, b in enumerate((2 * zh, 2 * zh + 1))
        ]
        for yh in range(y // 2)
        for zh in range(z // 2)
        for core in range(cores)
    ]


def local(psi, left_env, right_env, source, left_size, right_size):
    size = lax.axis_size
    rows = psi.shape[2]
    cols = psi.shape[3]
    near = size("yl") * size("zl")
    far = size("yh") * size("zh")
    each = rows // (near * far)

    def order(p):
        unit, last = p // each, p % each
        zh, unit = unit % size("zh"), unit // size("zh")
        yh, unit = unit % size("yh"), unit // size("yh")
        zl, yl = unit % size("zl"), unit // size("zl")
        term = ((yh * size("yl") + yl) * size("zh") + zh) * size("zl") + zl
        return term * each + last

    share = cols // near
    part = lax.axis_index("yl") * size("zl") + lax.axis_index("zl")
    turned = jnp.transpose(psi[:, 0], (0, 2, 1))
    mine = lax.dynamic_slice_in_dim(turned, part * share, share, 1)
    sends = jnp.broadcast_to(mine[None], (size("x"),) + mine.shape)
    sends = sends.reshape(-1, share, rows)
    peers = ("core", "yl", "zl")
    slots = size("core") * near
    asked = jnp.where(jnp.arange(slots) == lax.axis_index(peers), source.reshape(1), 0)
    left, right = left_env[0, 0], right_env[0, 0]
    sends, asked, left, right = lax.optimization_barrier((sends, asked, left, right))
    have = lax.all_to_all(sends, ("x", "core"), 0, 0)
    wanted = lax.psum(asked, peers)
    lefts, rights = prepare(order, source, left_size, right_size, left, right)
    block = lax.all_to_all(pick(have, wanted), peers, 0, 0)
    block = block.reshape(VECTORS * cols, rows)

    result = apply(block, lefts, rights)
    result = result.reshape(near, rows // near, VECTORS * cols)
    got = lax.all_to_all(result, ("yh", "yl", "zh", "zl", "core"), 0, 0, axis_index_groups=squares())
    total = jnp.sum(got.astype(jnp.float32), axis=0).astype(jnp.bfloat16)
    got = lax.all_to_all(total.reshape(far, each, VECTORS * cols), ("yh", "zh"), 0, 0)
    return finish(got)


def solution(mesh):
    y, z = 8, 16
    shape = (y // 2, 2, z // 2, 2, 4, 2)
    fine = Mesh(mesh.devices.reshape(shape), ("yh", "yl", "zh", "zl", "x", "core"))
    term = ("yh", "yl", "zh", "zl")
    blk = ("x", "core")
    return jax.shard_map(
        local,
        mesh=fine,
        in_specs=(P(None, blk), P(term, blk), P(term, blk), P(term, blk), P(), P()),
        out_specs=P(None, blk, term),
        check_vma=False,
    )
```

```python
import jax
import jax.numpy as jnp
from jax import lax
from jax.experimental import pallas as pl
from jax.experimental.pallas import tpu as pltpu
from jax.sharding import Mesh, PartitionSpec as P

VECTORS = 2


def pick_kernel(wanted, have, out):
    for i in range(out.shape[0]):
        out[i] = have[wanted[i]]


def pick(have, wanted):
    return pl.pallas_call(
        pick_kernel,
        out_shape=jax.ShapeDtypeStruct(have.shape, have.dtype),
        in_specs=[
            pl.BlockSpec(memory_space=pltpu.SMEM),
            pl.BlockSpec(memory_space=pltpu.VMEM),
        ],
        out_specs=pl.BlockSpec(memory_space=pltpu.VMEM),
        compiler_params=pltpu.CompilerParams(vmem_limit_bytes=16 * 1024 * 1024),
        name="pick",
    )(wanted, have)


def prepare_kernel(order, source, left_size, right_size, left, right, lefts, rights):
    rows = left.shape[0]
    cols = right.shape[0]
    here = lax.axis_index("x") * lax.axis_size("core") + lax.axis_index("core")
    target = source[0, 0]
    out_row = lax.broadcasted_iota(jnp.int32, (rows, rows), 0)
    in_row = lax.broadcasted_iota(jnp.int32, (rows, rows), 1)
    keep = (order(out_row) == in_row) & (in_row < left_size[here])
    permute = jnp.where(keep, 1.0, 0.0).astype(left.dtype)
    live = in_row < left_size[target]
    masked = jnp.where(live, left[...], jnp.zeros_like(left))
    lefts[...] = jnp.dot(permute, masked, preferred_element_type=jnp.float32).astype(left.dtype)
    row = lax.broadcasted_iota(jnp.int32, (cols, cols), 0)
    col = lax.broadcasted_iota(jnp.int32, (cols, cols), 1)
    live = (row < right_size[target]) & (col < right_size[here])
    rights[...] = jnp.where(live, right[...], jnp.zeros_like(right))


def prepare(order, source, left_size, right_size, left, right):
    smem = pl.BlockSpec(memory_space=pltpu.SMEM)
    vmem = pl.BlockSpec(memory_space=pltpu.VMEM)
    rows = left.shape[0]
    return pl.pallas_call(
        lambda *refs: prepare_kernel(order, *refs),
        out_shape=[jax.ShapeDtypeStruct(a.shape, a.dtype) for a in (left, right)],
        in_specs=[smem] * 3 + [vmem] * 2,
        out_specs=[vmem] * 2,
        compiler_params=pltpu.CompilerParams(vmem_limit_bytes=16 * 1024 * 1024),
        cost_estimate=pl.CostEstimate(flops=2 * rows**3, bytes_accessed=8 * rows * rows, transcendentals=0),
        name="prepare",
    )(source, left_size, right_size, left, right)


def apply_kernel(block, lefts, rights, out):
    cols = rights.shape[0]
    results = []
    for v in range(VECTORS):
        middle = lax.dot_general(
            lefts[...],
            block[v * cols : (v + 1) * cols, :],
            (((1,), (1,)), ((), ())),
            preferred_element_type=jnp.float32,
        ).astype(lefts.dtype)
        results.append(jnp.dot(middle, rights[...], preferred_element_type=jnp.float32))
    out[...] = jnp.concatenate(results, axis=1).astype(out.dtype)


def apply(block, lefts, rights):
    vmem = pl.BlockSpec(memory_space=pltpu.VMEM)
    return pl.pallas_call(
        apply_kernel,
        out_shape=jax.ShapeDtypeStruct((lefts.shape[0], VECTORS * rights.shape[1]), lefts.dtype),
        in_specs=[vmem] * 3,
        out_specs=vmem,
        compiler_params=pltpu.CompilerParams(vmem_limit_bytes=24 * 1024 * 1024),
        name="apply",
    )(block, lefts, rights)


def squares():
    y, z, cores = (lax.axis_size(("yh", "yl")), lax.axis_size(("zh", "zl")), lax.axis_size("core"))
    return [
        [
            (((a - 2 * core * yl) % y) * z + (b - 2 * core * zl) % z) * cores + core
            for yl, a in enumerate((2 * yh, 2 * yh + 1))
            for zl, b in enumerate((2 * zh, 2 * zh + 1))
        ]
        for yh in range(y // 2)
        for zh in range(z // 2)
        for core in range(cores)
    ]


def local(psi, left_env, right_env, source, left_size, right_size):
    size = lax.axis_size
    rows = psi.shape[2]
    cols = psi.shape[3]
    near = size("yl") * size("zl")
    far = size("yh") * size("zh")
    each = rows // (near * far)

    def order(p):
        unit, last = p // each, p % each
        zh, unit = unit % size("zh"), unit // size("zh")
        yh, unit = unit % size("yh"), unit // size("yh")
        zl, yl = unit % size("zl"), unit // size("zl")
        term = ((yh * size("yl") + yl) * size("zh") + zh) * size("zl") + zl
        return term * each + last

    share = cols // near
    part = lax.axis_index("yl") * size("zl") + lax.axis_index("zl")
    turned = jnp.transpose(psi[:, 0], (0, 2, 1))
    mine = lax.dynamic_slice_in_dim(turned, part * share, share, 1)
    sends = jnp.broadcast_to(mine[None], (size("x"),) + mine.shape)
    sends = sends.reshape(-1, share, rows)
    peers = ("core", "yl", "zl")
    slots = size("core") * near
    asked = jnp.where(jnp.arange(slots) == lax.axis_index(peers), source.reshape(1), 0)
    left, right = left_env[0, 0], right_env[0, 0]
    sends, asked, left, right = lax.optimization_barrier((sends, asked, left, right))
    have = lax.all_to_all(sends, ("x", "core"), 0, 0)
    wanted = lax.psum(asked, peers)
    lefts, rights = prepare(order, source, left_size, right_size, left, right)
    picked, lefts, rights = lax.optimization_barrier((pick(have, wanted), lefts, rights))
    block = lax.all_to_all(picked, peers, 0, 0)
    block = block.reshape(VECTORS * cols, rows)

    result = apply(block, lefts, rights)
    result = result.reshape(near, rows // near, VECTORS * cols)
    got = lax.all_to_all(result, ("yh", "yl", "zh", "zl", "core"), 0, 0, axis_index_groups=squares())
    total = jnp.sum(got.astype(jnp.float32), axis=0).astype(jnp.bfloat16)
    got = lax.all_to_all(total.reshape(far, each, VECTORS * cols), ("yh", "zh"), 0, 0)
    total = jnp.sum(got.astype(jnp.float32), axis=0)
    return jnp.transpose(total.reshape(each, VECTORS, cols), (1, 0, 2))[:, None]


def solution(mesh):
    y, z = 8, 16
    shape = (y // 2, 2, z // 2, 2, 4, 2)
    fine = Mesh(mesh.devices.reshape(shape), ("yh", "yl", "zh", "zl", "x", "core"))
    term = ("yh", "yl", "zh", "zl")
    blk = ("x", "core")
    return jax.shard_map(
        local,
        mesh=fine,
        in_specs=(P(None, blk), P(term, blk), P(term, blk), P(term, blk), P(), P()),
        out_specs=P(None, blk, term),
        check_vma=False,
    )
```

```python
import jax
import jax.numpy as jnp
from jax import lax
from jax.experimental import pallas as pl
from jax.experimental.pallas import tpu as pltpu
from jax.sharding import Mesh, PartitionSpec as P

VECTORS = 2
STRIDE = 19


def pick_kernel(wanted, have, out):
    for i in range(out.shape[0]):
        out[i] = have[wanted[i]]


def pick(have, wanted):
    return pl.pallas_call(
        pick_kernel,
        out_shape=jax.ShapeDtypeStruct(have.shape, have.dtype),
        in_specs=[
            pl.BlockSpec(memory_space=pltpu.SMEM),
            pl.BlockSpec(memory_space=pltpu.VMEM),
        ],
        out_specs=pl.BlockSpec(memory_space=pltpu.VMEM),
        compiler_params=pltpu.CompilerParams(vmem_limit_bytes=16 * 1024 * 1024),
        name="pick",
    )(wanted, have)


def prepare_kernel(order, source, left_size, right_size, left, right, lefts, rights):
    rows = left.shape[0]
    cols = right.shape[0]
    here = lax.axis_index("x") * lax.axis_size("core") + lax.axis_index("core")
    target = source[0, 0]
    out_row = lax.broadcasted_iota(jnp.int32, (rows, rows), 0)
    in_row = lax.broadcasted_iota(jnp.int32, (rows, rows), 1)
    keep = (order(out_row) == in_row) & (in_row < left_size[here])
    permute = jnp.where(keep, 1.0, 0.0).astype(left.dtype)
    live = in_row < left_size[target]
    masked = jnp.where(live, left[...], jnp.zeros_like(left))
    lefts[...] = jnp.dot(permute, masked, preferred_element_type=jnp.float32).astype(left.dtype)
    row = lax.broadcasted_iota(jnp.int32, (cols, cols), 0)
    col = lax.broadcasted_iota(jnp.int32, (cols, cols), 1)
    live = (row < right_size[target]) & (col < right_size[here])
    rights[...] = jnp.where(live, right[...], jnp.zeros_like(right))


def prepare(order, source, left_size, right_size, left, right):
    smem = pl.BlockSpec(memory_space=pltpu.SMEM)
    vmem = pl.BlockSpec(memory_space=pltpu.VMEM)
    rows = left.shape[0]
    return pl.pallas_call(
        lambda *refs: prepare_kernel(order, *refs),
        out_shape=[jax.ShapeDtypeStruct(a.shape, a.dtype) for a in (left, right)],
        in_specs=[smem] * 3 + [vmem] * 2,
        out_specs=[vmem] * 2,
        compiler_params=pltpu.CompilerParams(vmem_limit_bytes=16 * 1024 * 1024),
        cost_estimate=pl.CostEstimate(flops=2 * rows**3, bytes_accessed=8 * rows * rows, transcendentals=0),
        name="prepare",
    )(source, left_size, right_size, left, right)


def apply_kernel(block, lefts, rights, out):
    cols = rights.shape[0]
    results = []
    for v in range(VECTORS):
        middle = lax.dot_general(
            lefts[...],
            block[v * cols : (v + 1) * cols, :],
            (((1,), (1,)), ((), ())),
            preferred_element_type=jnp.float32,
        ).astype(lefts.dtype)
        results.append(jnp.dot(middle, rights[...], preferred_element_type=jnp.float32))
    out[...] = jnp.concatenate(results, axis=1).astype(out.dtype)


def apply(block, lefts, rights):
    vmem = pl.BlockSpec(memory_space=pltpu.VMEM)
    return pl.pallas_call(
        apply_kernel,
        out_shape=jax.ShapeDtypeStruct((lefts.shape[0], VECTORS * rights.shape[1]), lefts.dtype),
        in_specs=[vmem] * 3,
        out_specs=vmem,
        compiler_params=pltpu.CompilerParams(vmem_limit_bytes=24 * 1024 * 1024),
        name="apply",
    )(block, lefts, rights)


def squares():
    y, z, cores = (lax.axis_size(("yh", "yl")), lax.axis_size(("zh", "zl")), lax.axis_size("core"))
    return [
        [
            (((a - 2 * core * yl) % y) * z + (b - 2 * core * zl) % z) * cores + core
            for yl, a in enumerate((2 * yh, 2 * yh + 1))
            for zl, b in enumerate((2 * zh, 2 * zh + 1))
        ]
        for yh in range(y // 2)
        for zh in range(z // 2)
        for core in range(cores)
    ]


def chip_at(place):
    yh, zh = lax.axis_size("yh"), lax.axis_size("zh")
    number = place * STRIDE % (yh * zh)
    return number % yh, number // yh


def strides():
    z, cores = (lax.axis_size(("zh", "zl")), lax.axis_size("core"))
    far = lax.axis_size("yh") * lax.axis_size("zh")
    chips = [chip_at(place) for place in range(far)]
    return [
        [((2 * yh + yl) * z + 2 * zh + zl) * cores + core for yh, zh in chips]
        for yl in range(lax.axis_size("yl"))
        for zl in range(lax.axis_size("zl"))
        for core in range(cores)
    ]


def local(psi, left_env, right_env, source, left_size, right_size):
    size = lax.axis_size
    rows = psi.shape[2]
    cols = psi.shape[3]
    near = size("yl") * size("zl")
    far = size("yh") * size("zh")
    each = rows // (near * far)

    def order(p):
        unit, last = p // each, p % each
        yh, zh = chip_at(unit % far)
        zl, yl = unit // far % size("zl"), unit // far // size("zl")
        term = ((yh * size("yl") + yl) * size("zh") + zh) * size("zl") + zl
        return term * each + last

    share = cols // near
    part = lax.axis_index("yl") * size("zl") + lax.axis_index("zl")
    turned = jnp.transpose(psi[:, 0], (0, 2, 1))
    mine = lax.dynamic_slice_in_dim(turned, part * share, share, 1)
    sends = jnp.broadcast_to(mine[None], (size("x"),) + mine.shape)
    sends = sends.reshape(-1, share, rows)
    peers = ("core", "yl", "zl")
    slots = size("core") * near
    asked = jnp.where(jnp.arange(slots) == lax.axis_index(peers), source.reshape(1), 0)
    left, right = left_env[0, 0], right_env[0, 0]
    sends, asked, left, right = lax.optimization_barrier((sends, asked, left, right))
    have = lax.all_to_all(sends, ("x", "core"), 0, 0)
    wanted = lax.psum(asked, peers)
    lefts, rights = prepare(order, source, left_size, right_size, left, right)
    picked, lefts, rights = lax.optimization_barrier((pick(have, wanted), lefts, rights))
    block = lax.all_to_all(picked, peers, 0, 0)
    block = block.reshape(VECTORS * cols, rows)

    result = apply(block, lefts, rights)
    result = result.reshape(near, rows // near, VECTORS * cols)
    got = lax.all_to_all(result, ("yh", "yl", "zh", "zl", "core"), 0, 0, axis_index_groups=squares())
    total = jnp.sum(got.astype(jnp.float32), axis=0).astype(jnp.bfloat16)
    parts = total.reshape(far, each, VECTORS * cols)
    got = lax.all_to_all(parts, ("yh", "yl", "zh", "zl", "core"), 0, 0, axis_index_groups=strides())
    total = jnp.sum(got.astype(jnp.float32), axis=0)
    return jnp.transpose(total.reshape(each, VECTORS, cols), (1, 0, 2))[:, None]


def solution(mesh):
    y, z = 8, 16
    shape = (y // 2, 2, z // 2, 2, 4, 2)
    fine = Mesh(mesh.devices.reshape(shape), ("yh", "yl", "zh", "zl", "x", "core"))
    term = ("yh", "yl", "zh", "zl")
    blk = ("x", "core")
    return jax.shard_map(
        local,
        mesh=fine,
        in_specs=(P(None, blk), P(term, blk), P(term, blk), P(term, blk), P(), P()),
        out_specs=P(None, blk, term),
        check_vma=False,
    )
```

```python
import jax
import jax.numpy as jnp
from jax import lax
from jax.experimental import pallas as pl
from jax.experimental.pallas import tpu as pltpu
from jax.sharding import Mesh, PartitionSpec as P

VECTORS = 2
STRIDE = 29


def pick_kernel(wanted, have, out):
    for i in range(out.shape[0]):
        out[i] = have[wanted[i]]


def pick(have, wanted):
    return pl.pallas_call(
        pick_kernel,
        out_shape=jax.ShapeDtypeStruct(have.shape, have.dtype),
        in_specs=[
            pl.BlockSpec(memory_space=pltpu.SMEM),
            pl.BlockSpec(memory_space=pltpu.VMEM),
        ],
        out_specs=pl.BlockSpec(memory_space=pltpu.VMEM),
        compiler_params=pltpu.CompilerParams(vmem_limit_bytes=16 * 1024 * 1024),
        name="pick",
    )(wanted, have)


def prepare_kernel(order, source, left_size, right_size, left, right, lefts, rights):
    rows = left.shape[0]
    cols = right.shape[0]
    here = lax.axis_index("x") * lax.axis_size("core") + lax.axis_index("core")
    target = source[0, 0]
    out_row = lax.broadcasted_iota(jnp.int32, (rows, rows), 0)
    in_row = lax.broadcasted_iota(jnp.int32, (rows, rows), 1)
    keep = (order(out_row) == in_row) & (in_row < left_size[here])
    permute = jnp.where(keep, 1.0, 0.0).astype(left.dtype)
    live = in_row < left_size[target]
    masked = jnp.where(live, left[...], jnp.zeros_like(left))
    lefts[...] = jnp.dot(permute, masked, preferred_element_type=jnp.float32).astype(left.dtype)
    row = lax.broadcasted_iota(jnp.int32, (cols, cols), 0)
    col = lax.broadcasted_iota(jnp.int32, (cols, cols), 1)
    live = (row < right_size[target]) & (col < right_size[here])
    rights[...] = jnp.where(live, right[...], jnp.zeros_like(right))


def prepare(order, source, left_size, right_size, left, right):
    smem = pl.BlockSpec(memory_space=pltpu.SMEM)
    vmem = pl.BlockSpec(memory_space=pltpu.VMEM)
    rows = left.shape[0]
    return pl.pallas_call(
        lambda *refs: prepare_kernel(order, *refs),
        out_shape=[jax.ShapeDtypeStruct(a.shape, a.dtype) for a in (left, right)],
        in_specs=[smem] * 3 + [vmem] * 2,
        out_specs=[vmem] * 2,
        compiler_params=pltpu.CompilerParams(vmem_limit_bytes=16 * 1024 * 1024),
        cost_estimate=pl.CostEstimate(flops=2 * rows**3, bytes_accessed=8 * rows * rows, transcendentals=0),
        name="prepare",
    )(source, left_size, right_size, left, right)


def apply_kernel(block, lefts, rights, out):
    cols = rights.shape[0]
    results = []
    for v in range(VECTORS):
        middle = lax.dot_general(
            lefts[...],
            block[v * cols : (v + 1) * cols, :],
            (((1,), (1,)), ((), ())),
            preferred_element_type=jnp.float32,
        ).astype(lefts.dtype)
        results.append(jnp.dot(middle, rights[...], preferred_element_type=jnp.float32))
    out[...] = jnp.concatenate(results, axis=1).astype(out.dtype)


def apply(block, lefts, rights):
    vmem = pl.BlockSpec(memory_space=pltpu.VMEM)
    return pl.pallas_call(
        apply_kernel,
        out_shape=jax.ShapeDtypeStruct((lefts.shape[0], VECTORS * rights.shape[1]), lefts.dtype),
        in_specs=[vmem] * 3,
        out_specs=vmem,
        compiler_params=pltpu.CompilerParams(vmem_limit_bytes=24 * 1024 * 1024),
        name="apply",
    )(block, lefts, rights)


def squares():
    y, z, cores = (lax.axis_size(("yh", "yl")), lax.axis_size(("zh", "zl")), lax.axis_size("core"))
    return [
        [
            (((a - 2 * core * yl) % y) * z + (b - 2 * core * zl) % z) * cores + core
            for yl, a in enumerate((2 * yh, 2 * yh + 1))
            for zl, b in enumerate((2 * zh, 2 * zh + 1))
        ]
        for yh in range(y // 2)
        for zh in range(z // 2)
        for core in range(cores)
    ]


def chip_at(place):
    yh, zh = lax.axis_size("yh"), lax.axis_size("zh")
    number = place * STRIDE % (yh * zh)
    return number % yh, number // yh


def strides():
    z, cores = (lax.axis_size(("zh", "zl")), lax.axis_size("core"))
    far = lax.axis_size("yh") * lax.axis_size("zh")
    chips = [chip_at(place) for place in range(far)]
    return [
        [((2 * yh + yl) * z + 2 * zh + zl) * cores + core for yh, zh in chips]
        for yl in range(lax.axis_size("yl"))
        for zl in range(lax.axis_size("zl"))
        for core in range(cores)
    ]


def local(psi, left_env, right_env, source, left_size, right_size):
    size = lax.axis_size
    rows = psi.shape[2]
    cols = psi.shape[3]
    near = size("yl") * size("zl")
    far = size("yh") * size("zh")
    each = rows // (near * far)

    def order(p):
        unit, last = p // each, p % each
        yh, zh = chip_at(unit % far)
        zl, yl = unit // far % size("zl"), unit // far // size("zl")
        term = ((yh * size("yl") + yl) * size("zh") + zh) * size("zl") + zl
        return term * each + last

    share = cols // near
    part = lax.axis_index("yl") * size("zl") + lax.axis_index("zl")
    turned = jnp.transpose(psi[:, 0], (0, 2, 1))
    mine = lax.dynamic_slice_in_dim(turned, part * share, share, 1)
    sends = jnp.broadcast_to(mine[None], (size("x"),) + mine.shape)
    sends = sends.reshape(-1, share, rows)
    peers = ("core", "yl", "zl")
    slots = size("core") * near
    asked = jnp.where(jnp.arange(slots) == lax.axis_index(peers), source.reshape(1), 0)
    left, right = left_env[0, 0], right_env[0, 0]
    sends, asked, left, right = lax.optimization_barrier((sends, asked, left, right))
    have = lax.all_to_all(sends, ("x", "core"), 0, 0)
    wanted = lax.psum(asked, peers)
    lefts, rights = prepare(order, source, left_size, right_size, left, right)
    picked, lefts, rights = lax.optimization_barrier((pick(have, wanted), lefts, rights))
    block = lax.all_to_all(picked, peers, 0, 0)
    block = block.reshape(VECTORS * cols, rows)

    result = apply(block, lefts, rights)
    result = result.reshape(near, rows // near, VECTORS * cols)
    got = lax.all_to_all(result, ("yh", "yl", "zh", "zl", "core"), 0, 0, axis_index_groups=squares())
    total = jnp.sum(got.astype(jnp.float32), axis=0).astype(jnp.bfloat16)
    parts = total.reshape(far, each, VECTORS * cols)
    got = lax.all_to_all(parts, ("yh", "yl", "zh", "zl", "core"), 0, 0, axis_index_groups=strides())
    total = jnp.sum(got.astype(jnp.float32), axis=0)
    return jnp.transpose(total.reshape(each, VECTORS, cols), (1, 0, 2))[:, None]


def solution(mesh):
    y, z = 8, 16
    shape = (y // 2, 2, z // 2, 2, 4, 2)
    fine = Mesh(mesh.devices.reshape(shape), ("yh", "yl", "zh", "zl", "x", "core"))
    term = ("yh", "yl", "zh", "zl")
    blk = ("x", "core")
    return jax.shard_map(
        local,
        mesh=fine,
        in_specs=(P(None, blk), P(term, blk), P(term, blk), P(term, blk), P(), P()),
        out_specs=P(None, blk, term),
        check_vma=False,
    )
```

```python
import jax
import jax.numpy as jnp
from jax import lax
from jax.experimental import pallas as pl
from jax.experimental.pallas import tpu as pltpu
from jax.sharding import Mesh, PartitionSpec as P

VECTORS = 2
STRIDE = 29


def pick_kernel(wanted, have, out):
    for i in range(out.shape[0]):
        out[i] = have[wanted[i]]


def pick(have, wanted):
    return pl.pallas_call(
        pick_kernel,
        out_shape=jax.ShapeDtypeStruct(have.shape, have.dtype),
        in_specs=[
            pl.BlockSpec(memory_space=pltpu.SMEM),
            pl.BlockSpec(memory_space=pltpu.VMEM),
        ],
        out_specs=pl.BlockSpec(memory_space=pltpu.VMEM),
        compiler_params=pltpu.CompilerParams(vmem_limit_bytes=16 * 1024 * 1024),
        name="pick",
    )(wanted, have)


def prepare_kernel(order, source, left_size, right_size, left, right, lefts, rights):
    rows = left.shape[0]
    cols = right.shape[0]
    here = lax.axis_index("x") * lax.axis_size("core") + lax.axis_index("core")
    target = source[0, 0]
    out_row = lax.broadcasted_iota(jnp.int32, (rows, rows), 0)
    in_row = lax.broadcasted_iota(jnp.int32, (rows, rows), 1)
    keep = (order(out_row) == in_row) & (in_row < left_size[here])
    permute = jnp.where(keep, 1.0, 0.0).astype(left.dtype)
    live = in_row < left_size[target]
    masked = jnp.where(live, left[...], jnp.zeros_like(left))
    lefts[...] = jnp.dot(permute, masked, preferred_element_type=jnp.float32).astype(left.dtype)
    row = lax.broadcasted_iota(jnp.int32, (cols, cols), 0)
    col = lax.broadcasted_iota(jnp.int32, (cols, cols), 1)
    live = (row < right_size[target]) & (col < right_size[here])
    rights[...] = jnp.where(live, right[...], jnp.zeros_like(right))


def prepare(order, source, left_size, right_size, left, right):
    smem = pl.BlockSpec(memory_space=pltpu.SMEM)
    vmem = pl.BlockSpec(memory_space=pltpu.VMEM)
    rows = left.shape[0]
    return pl.pallas_call(
        lambda *refs: prepare_kernel(order, *refs),
        out_shape=[jax.ShapeDtypeStruct(a.shape, a.dtype) for a in (left, right)],
        in_specs=[smem] * 3 + [vmem] * 2,
        out_specs=[vmem] * 2,
        compiler_params=pltpu.CompilerParams(vmem_limit_bytes=16 * 1024 * 1024),
        cost_estimate=pl.CostEstimate(flops=2 * rows**3, bytes_accessed=8 * rows * rows, transcendentals=0),
        name="prepare",
    )(source, left_size, right_size, left, right)


def apply_kernel(block, lefts, rights, out):
    cols = rights.shape[0]
    results = []
    for v in range(VECTORS):
        middle = lax.dot_general(
            lefts[...],
            block[v * cols : (v + 1) * cols, :],
            (((1,), (1,)), ((), ())),
            preferred_element_type=jnp.float32,
        ).astype(lefts.dtype)
        results.append(jnp.dot(middle, rights[...], preferred_element_type=jnp.float32))
    out[...] = jnp.concatenate(results, axis=1).astype(out.dtype)


def apply(block, lefts, rights):
    vmem = pl.BlockSpec(memory_space=pltpu.VMEM)
    return pl.pallas_call(
        apply_kernel,
        out_shape=jax.ShapeDtypeStruct((lefts.shape[0], VECTORS * rights.shape[1]), lefts.dtype),
        in_specs=[vmem] * 3,
        out_specs=vmem,
        compiler_params=pltpu.CompilerParams(vmem_limit_bytes=24 * 1024 * 1024),
        name="apply",
    )(block, lefts, rights)


def squares():
    y, z, cores = (lax.axis_size(("yh", "yl")), lax.axis_size(("zh", "zl")), lax.axis_size("core"))
    return [
        [
            (((a - 2 * core * yl) % y) * z + (b - 2 * core * zl) % z) * cores + core
            for yl, a in enumerate((2 * yh, 2 * yh + 1))
            for zl, b in enumerate((2 * zh, 2 * zh + 1))
        ]
        for yh in range(y // 2)
        for zh in range(z // 2)
        for core in range(cores)
    ]


def chip_at(place):
    yh, zh = lax.axis_size("yh"), lax.axis_size("zh")
    number = place * STRIDE % (yh * zh)
    return number % yh, number // yh


def strides():
    z, cores = (lax.axis_size(("zh", "zl")), lax.axis_size("core"))
    far = lax.axis_size("yh") * lax.axis_size("zh")
    chips = [chip_at(place) for place in range(far)]
    return [
        [((2 * yh + yl) * z + 2 * zh + zl) * cores + core for yh, zh in chips]
        for yl in range(lax.axis_size("yl"))
        for zl in range(lax.axis_size("zl"))
        for core in range(cores)
    ]


def local(psi, left_env, right_env, source, left_size, right_size):
    size = lax.axis_size
    rows = psi.shape[2]
    cols = psi.shape[3]
    near = size("yl") * size("zl")
    far = size("yh") * size("zh")
    each = rows // (near * far)

    def order(p):
        unit, last = p // each, p % each
        yh, zh = chip_at(unit % far)
        zl, yl = unit // far % size("zl"), unit // far // size("zl")
        term = ((yh * size("yl") + yl) * size("zh") + zh) * size("zl") + zl
        return term * each + last

    share = cols // near
    part = lax.axis_index("yl") * size("zl") + lax.axis_index("zl")
    turned = jnp.transpose(psi[:, 0], (0, 2, 1))
    mine = lax.dynamic_slice_in_dim(turned, part * share, share, 1)
    sends = jnp.broadcast_to(mine[:, None], (size("core"), size("x"), share, rows))
    sends = sends.reshape(-1, share, rows)
    peers = ("core", "yl", "zl")
    slots = size("core") * near
    place = source.reshape(1) % size("core") * size("x") + source.reshape(1) // size("core")
    asked = jnp.where(jnp.arange(slots) == lax.axis_index(peers), place, 0)
    left, right = left_env[0, 0], right_env[0, 0]
    sends, asked, left, right = lax.optimization_barrier((sends, asked, left, right))
    have = lax.all_to_all(sends, ("core", "x"), 0, 0)
    wanted = lax.psum(asked, peers)
    lefts, rights = prepare(order, source, left_size, right_size, left, right)
    picked, lefts, rights = lax.optimization_barrier((pick(have, wanted), lefts, rights))
    block = lax.all_to_all(picked, peers, 0, 0)
    block = block.reshape(VECTORS * cols, rows)

    result = apply(block, lefts, rights)
    result = result.reshape(near, rows // near, VECTORS * cols)
    got = lax.all_to_all(result, ("yh", "yl", "zh", "zl", "core"), 0, 0, axis_index_groups=squares())
    total = jnp.sum(got.astype(jnp.float32), axis=0).astype(jnp.bfloat16)
    parts = total.reshape(far, each, VECTORS * cols)
    got = lax.all_to_all(parts, ("yh", "yl", "zh", "zl", "core"), 0, 0, axis_index_groups=strides())
    total = jnp.sum(got.astype(jnp.float32), axis=0)
    return jnp.transpose(total.reshape(each, VECTORS, cols), (1, 0, 2))[:, None]


def solution(mesh):
    y, z = 8, 16
    shape = (y // 2, 2, z // 2, 2, 4, 2)
    fine = Mesh(mesh.devices.reshape(shape), ("yh", "yl", "zh", "zl", "x", "core"))
    term = ("yh", "yl", "zh", "zl")
    blk = ("x", "core")
    return jax.shard_map(
        local,
        mesh=fine,
        in_specs=(P(None, blk), P(term, blk), P(term, blk), P(term, blk), P(), P()),
        out_specs=P(None, blk, term),
        check_vma=False,
    )
```

```python
import jax
import jax.numpy as jnp
from jax import lax
from jax.experimental import pallas as pl
from jax.experimental.pallas import tpu as pltpu
from jax.sharding import Mesh, PartitionSpec as P

VECTORS = 2
STRIDE = 25


def pick_kernel(wanted, have, out):
    for i in range(out.shape[0]):
        out[i] = have[wanted[i]]


def pick(have, wanted):
    return pl.pallas_call(
        pick_kernel,
        out_shape=jax.ShapeDtypeStruct(have.shape, have.dtype),
        in_specs=[
            pl.BlockSpec(memory_space=pltpu.SMEM),
            pl.BlockSpec(memory_space=pltpu.VMEM),
        ],
        out_specs=pl.BlockSpec(memory_space=pltpu.VMEM),
        compiler_params=pltpu.CompilerParams(vmem_limit_bytes=16 * 1024 * 1024),
        name="pick",
    )(wanted, have)


def prepare_kernel(order, source, left_size, right_size, left, right, lefts, rights):
    rows = left.shape[0]
    cols = right.shape[0]
    here = lax.axis_index("x") * lax.axis_size("core") + lax.axis_index("core")
    target = source[0, 0]
    out_row = lax.broadcasted_iota(jnp.int32, (rows, rows), 0)
    in_row = lax.broadcasted_iota(jnp.int32, (rows, rows), 1)
    keep = (order(out_row) == in_row) & (in_row < left_size[here])
    permute = jnp.where(keep, 1.0, 0.0).astype(left.dtype)
    live = in_row < left_size[target]
    masked = jnp.where(live, left[...], jnp.zeros_like(left))
    lefts[...] = jnp.dot(permute, masked, preferred_element_type=jnp.float32).astype(left.dtype)
    row = lax.broadcasted_iota(jnp.int32, (cols, cols), 0)
    col = lax.broadcasted_iota(jnp.int32, (cols, cols), 1)
    live = (row < right_size[target]) & (col < right_size[here])
    rights[...] = jnp.where(live, right[...], jnp.zeros_like(right))


def prepare(order, source, left_size, right_size, left, right):
    smem = pl.BlockSpec(memory_space=pltpu.SMEM)
    vmem = pl.BlockSpec(memory_space=pltpu.VMEM)
    rows = left.shape[0]
    return pl.pallas_call(
        lambda *refs: prepare_kernel(order, *refs),
        out_shape=[jax.ShapeDtypeStruct(a.shape, a.dtype) for a in (left, right)],
        in_specs=[smem] * 3 + [vmem] * 2,
        out_specs=[vmem] * 2,
        compiler_params=pltpu.CompilerParams(vmem_limit_bytes=16 * 1024 * 1024),
        cost_estimate=pl.CostEstimate(flops=2 * rows**3, bytes_accessed=8 * rows * rows, transcendentals=0),
        name="prepare",
    )(source, left_size, right_size, left, right)


def apply_kernel(block, lefts, rights, out):
    cols = rights.shape[0]
    results = []
    for v in range(VECTORS):
        middle = lax.dot_general(
            lefts[...],
            block[v * cols : (v + 1) * cols, :],
            (((1,), (1,)), ((), ())),
            preferred_element_type=jnp.float32,
        ).astype(lefts.dtype)
        results.append(jnp.dot(middle, rights[...], preferred_element_type=jnp.float32))
    out[...] = jnp.concatenate(results, axis=1).astype(out.dtype)


def apply(block, lefts, rights):
    vmem = pl.BlockSpec(memory_space=pltpu.VMEM)
    return pl.pallas_call(
        apply_kernel,
        out_shape=jax.ShapeDtypeStruct((lefts.shape[0], VECTORS * rights.shape[1]), lefts.dtype),
        in_specs=[vmem] * 3,
        out_specs=vmem,
        compiler_params=pltpu.CompilerParams(vmem_limit_bytes=24 * 1024 * 1024),
        name="apply",
    )(block, lefts, rights)


def squares():
    y, z, cores = (lax.axis_size(("yh", "yl")), lax.axis_size(("zh", "zl")), lax.axis_size("core"))
    return [
        [
            (((a - 2 * core * yl) % y) * z + (b - 2 * core * zl) % z) * cores + core
            for yl, a in enumerate((2 * yh, 2 * yh + 1))
            for zl, b in enumerate((2 * zh, 2 * zh + 1))
        ]
        for yh in range(y // 2)
        for zh in range(z // 2)
        for core in range(cores)
    ]


def chip_at(place):
    yh, zh = lax.axis_size("yh"), lax.axis_size("zh")
    number = place * STRIDE % (yh * zh)
    return number % yh, number // yh


def strides():
    z, cores = (lax.axis_size(("zh", "zl")), lax.axis_size("core"))
    far = lax.axis_size("yh") * lax.axis_size("zh")
    chips = [chip_at(place) for place in range(far)]
    return [
        [((2 * yh + yl) * z + 2 * zh + zl) * cores + core for yh, zh in chips]
        for yl in range(lax.axis_size("yl"))
        for zl in range(lax.axis_size("zl"))
        for core in range(cores)
    ]


def local(psi, left_env, right_env, source, left_size, right_size):
    size = lax.axis_size
    rows = psi.shape[2]
    cols = psi.shape[3]
    near = size("yl") * size("zl")
    far = size("yh") * size("zh")
    each = rows // (near * far)

    def order(p):
        unit, last = p // each, p % each
        yh, zh = chip_at(unit % far)
        zl, yl = unit // far % size("zl"), unit // far // size("zl")
        term = ((yh * size("yl") + yl) * size("zh") + zh) * size("zl") + zl
        return term * each + last

    share = cols // near
    part = lax.axis_index("yl") * size("zl") + lax.axis_index("zl")
    turned = jnp.transpose(psi[:, 0], (0, 2, 1))
    mine = lax.dynamic_slice_in_dim(turned, part * share, share, 1)
    sends = jnp.broadcast_to(mine[:, None], (size("core"), size("x"), share, rows))
    sends = sends.reshape(-1, share, rows)
    peers = ("core", "yl", "zl")
    slots = size("core") * near
    place = source.reshape(1) % size("core") * size("x") + source.reshape(1) // size("core")
    asked = jnp.where(jnp.arange(slots) == lax.axis_index(peers), place, 0)
    left, right = left_env[0, 0], right_env[0, 0]
    sends, asked, left, right = lax.optimization_barrier((sends, asked, left, right))
    have = lax.all_to_all(sends, ("core", "x"), 0, 0)
    wanted = lax.psum(asked, peers)
    lefts, rights = prepare(order, source, left_size, right_size, left, right)
    picked, lefts, rights = lax.optimization_barrier((pick(have, wanted), lefts, rights))
    block = lax.all_to_all(picked, peers, 0, 0)
    block = block.reshape(VECTORS * cols, rows)

    result = apply(block, lefts, rights)
    result = result.reshape(near, rows // near, VECTORS * cols)
    got = lax.all_to_all(result, ("yh", "yl", "zh", "zl", "core"), 0, 0, axis_index_groups=squares())
    total = jnp.sum(got.astype(jnp.float32), axis=0).astype(jnp.bfloat16)
    parts = total.reshape(far, each, VECTORS * cols)
    got = lax.all_to_all(parts, ("yh", "yl", "zh", "zl", "core"), 0, 0, axis_index_groups=strides())
    total = jnp.sum(got.astype(jnp.float32), axis=0)
    return jnp.transpose(total.reshape(each, VECTORS, cols), (1, 0, 2))[:, None]


def solution(mesh):
    y, z = 8, 16
    shape = (y // 2, 2, z // 2, 2, 4, 2)
    fine = Mesh(mesh.devices.reshape(shape), ("yh", "yl", "zh", "zl", "x", "core"))
    term = ("yh", "yl", "zh", "zl")
    blk = ("x", "core")
    return jax.shard_map(
        local,
        mesh=fine,
        in_specs=(P(None, blk), P(term, blk), P(term, blk), P(term, blk), P(), P()),
        out_specs=P(None, blk, term),
        check_vma=False,
    )
```
